32 devices in a mesh: energy: 4 (over z), slab: 8 (over y, x, core).
Axes of the slice: x: 2, y: 2, z: 4, core: 2. Of those that a mesh axis runs over, the one named last changes fastest.
Arguments:
- wavefunction: bfloat16 [4, 128, 64, 256], P('energy', 'slab'), may hold values from -6 to 6
- injected_modes: int32 [4, 64], P('energy'), may hold values from 0 to 255, all different within a row
- factor_blocks: float32 [4, 128, 256, 256], P('energy', 'slab'), may hold values from -1.1 to 1.1
- pivot_inverse: float32 [4, 128, 256, 256], P('energy', 'slab'), may hold values from -1 to 2.5
- mode_velocity: float32 [4, 256], P('energy'), may hold values from 0.1 to 1
- energy_weight: float32 [4], P('energy'), may hold values from 0.5 to 8
- mode_basis: bfloat16 [256, 1024], replicated, may hold values from -0.375 to 0.375
Outputs:
- sensitivity: float32 [1024, 128], P('energy', 'slab')
The draws below stay inside these ranges and needn't reach their ends.
Inputs may be any that keep to these rules, and one draw needn't show every extreme that they name: `injected_modes`: each energy's row names 64 different modes, and every mode is named by some energy.
All inputs are finite; a program needn't handle non-finite values.
Results may differ from the reference program's by a relative error of at most 0.0003.
Values sent between devices are 32-bit elements; how exact they have to be, the bound alone decides.
A program may use at most 128 MiB of HBM per device.

```python
import math
import jax
import jax.numpy as jnp
from jax import lax

M = 256
C = 64
G = 1024
SLAB_DEV = 16
ENERGY_GROUPS = 4
WIRE_SLABS = 128


def draw_factor_blocks(key, part):
    random_keys = jax.random.split(key, 7)
    slow_share = 0.5
    sluggish_part = jax.random.uniform(random_keys[0], (ENERGY_GROUPS, 1, M)) < slow_share
    fast_length = SLAB_DEV * jax.random.uniform(random_keys[1], (ENERGY_GROUPS, 1, M), minval=2.0, maxval=3.0)
    slow_length = WIRE_SLABS * jax.random.uniform(random_keys[2], (ENERGY_GROUPS, 1, M), minval=1.0, maxval=3.0)
    length = jnp.where(sluggish_part, slow_length, fast_length)
    spread = jnp.exp(jax.random.uniform(random_keys[3], (ENERGY_GROUPS, WIRE_SLABS, M), minval=-0.35, maxval=0.35))
    damping_rate = jnp.exp(-spread / length)
    sudden_spike = jax.random.uniform(random_keys[4], (ENERGY_GROUPS, WIRE_SLABS, 1)) < 3.0 / WIRE_SLABS
    loss_values = jax.random.uniform(random_keys[5], (ENERGY_GROUPS, WIRE_SLABS, M), minval=0.5, maxval=0.8)
    damping_rate = damping_rate * jnp.where(jnp.logical_and(sudden_spike, sluggish_part), loss_values, 1.0)
    mixing = jnp.clip(jax.random.normal(random_keys[6], (ENERGY_GROUPS, WIRE_SLABS, M, M)), -4.0, 4.0) * (0.1 / math.sqrt(M))
    return mixing + jnp.eye(M, dtype=jnp.float32) * damping_rate[..., None]


def draw_pivot_inverse(key, part):
    random_keys = jax.random.split(key, 2)
    diagonal = jax.random.uniform(random_keys[0], (ENERGY_GROUPS, WIRE_SLABS, M), minval=0.5, maxval=1.5)
    mixing = jnp.clip(jax.random.normal(random_keys[1], (ENERGY_GROUPS, WIRE_SLABS, M, M)), -4.0, 4.0) * (0.3 / math.sqrt(M))
    return mixing + jnp.eye(M, dtype=jnp.float32) * diagonal[..., None]


def draw_wavefunction(key, part):
    position = jnp.arange(WIRE_SLABS, dtype=jnp.float32) / WIRE_SLABS
    amplitude = (0.5 + position)[None, :, None, None]
    values = jnp.clip(jax.random.normal(key, (ENERGY_GROUPS, WIRE_SLABS, C, M)), -4.0, 4.0) * amplitude
    return values.astype(jnp.bfloat16)


def draw_energy_weight(key, part):
    level = jnp.arange(ENERGY_GROUPS, dtype=jnp.float32) / max(ENERGY_GROUPS - 1, 1)
    values = (1.0 + 2.0 * level) * jnp.exp(jax.random.uniform(key, (ENERGY_GROUPS,), minval=-0.2, maxval=0.2))
    return values


def shard_levels(key, dims, cuts, least, largest):
    def one(axis_at, shards_of):
        heights = jax.random.uniform(jax.random.fold_in(jax.random.fold_in(key, 6), axis_at), (shards_of,), jnp.float32, least / len(cuts), largest / len(cuts))
        return jnp.repeat(jnp.exp(heights), dims[axis_at] // shards_of).reshape((-1,) + (1,) * (len(dims) - axis_at - 1))

    factor_of = one(*cuts[0])
    for cut in cuts[1:]:
        factor_of = factor_of * one(*cut)
    return factor_of


def distinct(key, rows, amount, top, lift):
    ranking = jax.random.permutation(jax.random.fold_in(key, 1), amount)
    pull = ranking
    for power in range(3):
        pull = pull * pull // amount
    pull = pull * lift // amount
    chance = jax.random.randint(jax.random.fold_in(key, 2), (rows, amount), 0, 4096) + pull
    sure = jax.random.permutation(jax.random.fold_in(key, 3), rows)[jnp.arange(amount) % rows]
    chance = jnp.where(jnp.arange(rows)[:, None] == sure[None, :], 1 << 14, chance)
    merit = chance * amount + jnp.arange(amount)
    return lax.top_k(merit.astype(jnp.int32), top)[1].astype(jnp.int32)


def gaussian(own_key, dims, scale, bound, held_as=jnp.bfloat16):
    drawn = scale * jax.random.normal(own_key, dims, jnp.float32)
    return jnp.clip(drawn, min=-bound, max=bound).astype(held_as)


def setup_inputs(seed: int = 0) -> dict:
    streams_of = jax.random.split(jax.random.key(seed), 8)
    return {
        "wavefunction": draw_wavefunction(jax.random.fold_in(streams_of[7], 71), 0),
        "injected_modes": distinct(streams_of[1], ENERGY_GROUPS, M, C, 0),
        "factor_blocks": draw_factor_blocks(jax.random.fold_in(streams_of[7], 71), 0),
        "pivot_inverse": draw_pivot_inverse(jax.random.fold_in(streams_of[7], 71), 0),
        "mode_velocity": jnp.clip(jnp.exp(math.log(1.0) - 2.3025851 * jax.random.uniform(streams_of[4], (ENERGY_GROUPS, M), jnp.float32) ** shard_levels(streams_of[4], (ENERGY_GROUPS, M), ((0, 4),), -0.2, 0.2)), 0.1, 1.0),
        "energy_weight": draw_energy_weight(jax.random.fold_in(streams_of[7], 71), 0),
        "mode_basis": gaussian(streams_of[6], (M, G), M ** -0.5, 0.375),
    }


def reference(wavefunction, injected_modes, factor_blocks, pivot_inverse, mode_velocity, energy_weight, mode_basis):
    highest = lax.Precision.HIGHEST
    picked = jnp.take_along_axis(mode_velocity, injected_modes.astype(jnp.int32), axis=1)
    column_weight = 1.0 / picked
    wave_float = wavefunction.astype(jnp.float32)
    scaled = energy_weight[:, None, None] * column_weight[:, :, None] * mode_velocity[:, None, :]
    current = jnp.sum(scaled[:, None] * wave_float * wave_float) / WIRE_SLABS
    basis_float = mode_basis.astype(jnp.float32)
    empty = jnp.zeros((C, M), jnp.float32)

    def forward_step(carried, pieces):
        source_row, factor, pivot_block = pieces
        current_state = source_row + carried
        return (jnp.dot(current_state, factor, precision=highest, preferred_element_type=jnp.float32),
                jnp.dot(current_state, pivot_block, precision=highest, preferred_element_type=jnp.float32))

    def backward_step(carried, pieces):
        weighted_row, factor = pieces
        current_state = weighted_row + jnp.dot(carried, factor.T, precision=highest, preferred_element_type=jnp.float32)
        return current_state, current_state

    total_grad = jnp.zeros((WIRE_SLABS, G), jnp.float32)
    for energy in range(ENERGY_GROUPS):
        source = (2.0 / (WIRE_SLABS * current)) * scaled[energy][None] * wave_float[energy]
        weighted = lax.scan(forward_step, empty, (source, factor_blocks[energy], pivot_inverse[energy]))[1]
        adjoint = lax.scan(backward_step, empty, (weighted, factor_blocks[energy]), reverse=True)[1]
        wave_grid = jnp.dot(wavefunction[energy].reshape(WIRE_SLABS * C, M), mode_basis, preferred_element_type=jnp.float32)
        adjoint_grid = jnp.dot(adjoint.reshape(WIRE_SLABS * C, M), basis_float, precision=highest, preferred_element_type=jnp.float32)
        total_grad = total_grad + jnp.sum((wave_grid * adjoint_grid).reshape(WIRE_SLABS, C, G), axis=1)
    return (WIRE_SLABS * G) * total_grad.T
```

```python
import functools
import jax
import jax.numpy as jnp
from jax import lax
from jax.experimental import pallas as pl
from jax.experimental.pallas import tpu as pltpu
from jax.sharding import PartitionSpec as P

F32 = jnp.float32
BF16 = jnp.bfloat16
MESH = pl.DeviceIdType.MESH


def split(x):
    hi = x.astype(BF16)
    return hi, (x - hi.astype(F32)).astype(BF16)


def dot(a, b, transposed=False):
    return lax.dot_general(
        a, b, (((1,), (1 if transposed else 0,)), ((), ())), preferred_element_type=F32
    )


def mm_split(ah, al, bh, bl, transposed=False):
    rows = ah.shape[0]
    both = dot(jnp.concatenate([ah, al], axis=0), bh, transposed)
    return both[:rows] + both[rows:] + dot(ah, bl, transposed)


def mm(a, bh, bl, transposed=False):
    ah, al = split(a)
    return mm_split(ah, al, bh, bl, transposed)


def kernel(
    n, groups,
    wave, inj, fac_hbm, piv_hbm, vel, ew, basis,
    out,
    fac, piv, ahl, fac_sem, piv_sem,
    fh, fl, uh, ul, vh, vl, th, tl, zh, zl, wh, wl, gh, gl, ch, cl, srh, srl,
    state, rest, adj, wg, off, scaled_ref, whole_off, chip_off, local_e, exit_own,
    inc, incb, cinc, cur,
    po_s, po_r, pu_s, pu_r, pg_s, pg_r, osend, orecv, tsend, trecv, urecv, csend, crecv,
    isend, irecv, ysend, yrecv, jsend, jrecv, zsend, zrecv, ssend, srecv, esend, erecv,
    pos, por, pus, pur, pgs, pgr, os, our, us, ur, ts, tr, cs, cr, is_, ir, ys, yr, js, jr,
    zs, zr, ss, sr, es, er,
):
    me = lax.axis_index("slab")
    mine = lax.axis_index("energy")
    slabs, cols, modes = wave.shape
    grid = basis.shape[1]
    part = grid // groups
    chips = n // 2
    chip = me // 2
    core = lax.rem(me, 2)
    other = me + 1 - 2 * core
    odd = lax.rem(chip, 2)
    half = slabs // 2
    all_slabs = n * slabs
    small = 2.0 / (all_slabs * cols * modes * groups * 4096.0)

    def factor_in(s):
        return pltpu.make_async_copy(fac_hbm.at[s], fac.at[s], fac_sem.at[s])

    for i in range(half // 2):
        for k in range(2):
            factor_in(k * half + i).start()
            factor_in(k * half + half - 1 - i).start()
    pivots_in = pltpu.make_async_copy(piv_hbm, piv, piv_sem)
    pivots_in.start()

    barrier = pltpu.get_barrier_semaphore()

    for k in range(1, n):
        pl.semaphore_signal(
            barrier, inc=1, device_id=(mine, lax.rem(me + k, n)), device_id_type=MESH
        )
    for k in range(1, groups):
        peer = lax.rem(mine + k, groups)
        pl.semaphore_signal(barrier, inc=1, device_id=(peer, me), device_id_type=MESH)

    rows_at = lax.broadcasted_iota(jnp.int32, (cols, cols), 0)
    cols_at = lax.broadcasted_iota(jnp.int32, (cols, cols), 1)
    picked = jnp.sum(
        jnp.where(rows_at == cols_at, jnp.broadcast_to(inj[...].astype(F32), (cols, cols)), 0.0),
        axis=1, keepdims=True,
    )
    mode_at = lax.broadcasted_iota(jnp.int32, (cols, modes), 1).astype(F32)
    velocity = jnp.broadcast_to(vel[...], (cols, modes))
    at_injected = jnp.sum(jnp.where(mode_at == picked, velocity, 0.0), axis=1, keepdims=True)
    scaled_ref[...] = ew[...] * (1.0 / at_injected) * velocity

    eye = (
        lax.broadcasted_iota(jnp.int32, (modes, modes), 0)
        == lax.broadcasted_iota(jnp.int32, (modes, modes), 1)
    ).astype(F32).astype(BF16)

    for k in range(2):
        ch[k] = eye
        cl[k] = jnp.zeros((modes, modes), BF16)
        off[k] = jnp.zeros((cols, modes), F32)
    cur[...] = jnp.zeros_like(cur)

    def chain(i, carry):
        moved = []
        for k in range(2):
            s = k * half + i
            w = wave[s].astype(F32)
            sw = scaled_ref[...] * w
            sq = sw * w
            part_sum = sq[0:8]
            for j in range(1, cols // 8):
                part_sum = part_sum + sq[8 * j : 8 * j + 8]
            tile = part_sum[:, 0:128]
            for j in range(1, modes // 128):
                tile = tile + part_sum[:, 128 * j : 128 * j + 128]
            cur[...] += tile
            source = sw * small
            h, l = split(source)
            srh[s] = h
            srl[s] = l
            own = off[k] + source
            state[s] = own
            back = k * half + half - 1 - i
            moved.append(mm_split(ch[k], cl[k], fh[back], fl[back], True))
            moved.append(mm(own, fh[s], fl[s]))
        for k in range(2):
            back = k * half + half - 1 - i
            h, l = split(moved[2 * k])
            ch[k] = h
            cl[k] = l
            uh[back] = h
            ul[back] = l
            off[k] = moved[2 * k + 1]
        return carry

    def chain_in(i, carry):
        for k in range(2):
            for s in (k * half + i, k * half + half - 1 - i):
                factor_in(s).wait()
                h, l = split(fac[s])
                fh[s] = h
                fl[s] = l
        return chain(i, carry)

    lax.fori_loop(0, half // 2, chain_in, 0, unroll=2)
    lax.fori_loop(half // 2, half, chain, 0, unroll=2)

    def copy_to(source, target, send, receive, device):
        return pltpu.make_async_remote_copy(
            src_ref=source, dst_ref=target, send_sem=send, recv_sem=receive,
            device_id=(mine, device), device_id_type=MESH,
        )

    pair_off = copy_to(po_s, po_r, pos, por, other)
    pair_u = copy_to(pu_s, pu_r, pus, pur, other)
    pair_g = copy_to(pg_s, pg_r, pgs, pgr, other)
    entry = copy_to(isend, irecv, is_, ir, other)
    joining = copy_to(jsend, jrecv, js, jr, other)

    def chip_at(j):
        return 2 * lax.rem(j, chips) + 1

    offset_on = copy_to(osend, orecv, os, our, chip_at(chip + 1))
    transfer_on = copy_to(tsend, urecv, us, ur, chip_at(chip + 1))

    def carried_to(k):
        return copy_to(csend, crecv, cs.at[k], cr, chip_at(chip + 1 + k))

    def transfer_to(j):
        return copy_to(tsend, trecv.at[chip], ts.at[j], tr.at[chip], 2 * j + 1)

    def exit_to(j):
        return copy_to(ysend, yrecv.at[chip], ys.at[j], yr.at[chip], 2 * j + 1)

    def wait_transfer(j):
        copy_to(tsend, trecv.at[j], ts.at[j], tr.at[j], other).wait_recv()

    def wait_exit(j):
        copy_to(ysend, yrecv.at[j], ys.at[j], yr.at[j], other).wait_recv()

    def tile_to(k):
        peer = lax.rem(mine + k, groups)
        return pltpu.make_async_remote_copy(
            src_ref=zsend, dst_ref=zrecv.at[k], send_sem=zs.at[k], recv_sem=zr.at[k],
            device_id=(peer, me), device_id_type=MESH,
        )

    def share_to(d):
        return copy_to(ssend, srecv.at[chip], ss.at[d], sr.at[chip], d)

    inner = jnp.logical_and(chip > 0, chip < chips - 1)
    onward = jnp.logical_and(odd == 0, chip < chips - 1)

    off_a = off[0]
    whole_off[...] = mm(off_a, uh[half], ul[half], True) + off[1]
    po_s[0:cols] = whole_off[...]
    po_s[cols:, 0:128] = cur[...]
    po_s[cols:, 128:] = jnp.zeros((8, modes - 128), F32)

    pl.semaphore_wait(barrier, n + groups - 2)

    @pl.when(core == 0)
    def _():
        pair_off.start()

    whole = mm_split(uh[half], ul[half], uh[0], ul[0])
    h, l = split(whole)
    th[...] = h
    tl[...] = l

    @pl.when(core == 0)
    def _():
        pu_s[...] = whole
        pair_u.start()

    @pl.when(core == 1)
    def _():
        pair_off.wait_recv()
        chip_off[...] = mm(po_r[0:cols], th[...], tl[...], True) + whole_off[...]

        @pl.when(onward)
        def _():
            osend[...] = chip_off[...]
            offset_on.start()

        zsend[...] = cur[...] + po_r[cols:, 0:128]
        for k in range(1, groups):
            tile_to(k).start()
        pair_u.wait_recv()
        h, l = split(pu_r[...])
        zh[...] = h
        zl[...] = l
        joined = mm_split(th[...], tl[...], h, l)
        tsend[...] = joined

        @pl.when(jnp.logical_and(onward, chip > 0))
        def _():
            transfer_on.start()

        h, l = split(joined)
        wh[...] = h
        wl[...] = l

    pivots_in.wait()
    for k in range(2):
        end = k * half + half - 1
        h, l = split(piv[end])
        vh[end] = h
        vl[end] = l
        rest[end] = jnp.zeros((cols, modes), F32)

    def climb(i, carry):
        firsts = []
        for k in range(2):
            s = k * half + half - 2 - i
            first = mm_split(
                jnp.concatenate([fh[s], srh[s + 1]], axis=0),
                jnp.concatenate([fl[s], srl[s + 1]], axis=0),
                vh[s + 1], vl[s + 1],
            )
            firsts.append(jnp.concatenate([first[0:modes], first[modes:] + rest[s + 1]], axis=0))
        seconds = []
        for k in range(2):
            s = k * half + half - 2 - i
            seconds.append(mm(firsts[k], fh[s], fl[s], True))
        for k in range(2):
            s = k * half + half - 2 - i
            h, l = split(piv[s] + seconds[k][0:modes])
            vh[s] = h
            vl[s] = l
            rest[s] = seconds[k][modes:]
        return carry

    early = (half - 1) // 2
    lax.fori_loop(0, early, climb, 0)

    def carry_on():
        csend[...] = mm(cinc[...], wh[...], wl[...], True) + chip_off[...]
        carried_to(0).start()

        @pl.when(chip < chips - 2)
        def _():
            carried_to(1).start()

    cinc[...] = jnp.zeros_like(cinc)

    @pl.when(core == 1)
    def _():
        @pl.when(chip == 1)
        def _():
            offset_on.wait_recv()
            cinc[...] = orecv[...]
            if chips > 2:
                carry_on()

        @pl.when(inner)
        def _():
            for j in range(chips):
                @pl.when(j < chip)
                def _():
                    transfer_to(j).start()

    lax.fori_loop(early, half - 1, climb, 0)

    lead_h = dot(eye, uh[0], True).astype(BF16)
    lead_l = dot(eye, ul[0], True).astype(BF16)
    row_h, row_l = split(state[half] + off_a)
    first = mm_split(
        jnp.concatenate([lead_h, row_h], axis=0),
        jnp.concatenate([lead_l, row_l], axis=0),
        vh[half], vl[half],
    )
    first = jnp.concatenate([first[0:modes], first[modes:] + rest[half]], axis=0)
    second = mm(first, uh[0], ul[0])
    own_g = second[0:modes] + vh[0].astype(F32) + vl[0].astype(F32)
    own_e = second[modes:] + rest[0] + mm_split(srh[0], srl[0], vh[0], vl[0])

    @pl.when(core == 0)
    def _():
        pg_s[0:modes] = own_g
        pg_s[modes:] = own_e
        pair_g.start()
        entry.wait_recv()
        inc[...] = irecv[...]

    @pl.when(core == 1)
    def _():
        h, l = split(own_g)
        gh[...] = h
        gl[...] = l
        local_e[...] = own_e

        @pl.when(chip > 1)
        def _():
            carried_to(0).wait_recv()
            cinc[...] = crecv[...]

            @pl.when(odd == 1)
            def _():
                offset_on.wait_recv()
                transfer_on.wait_recv()
                h, l = split(urecv[...])
                cinc[...] = mm(cinc[...], h, l, True) + orecv[...]

                @pl.when(chip < chips - 1)
                def _():
                    carry_on()

        isend[...] = cinc[...]
        entry.start()
        inc[...] = mm(cinc[...], zh[...], zl[...], True) + po_r[0:cols]
        exit_own[...] = local_e[...] + mm(inc[...], gh[...], gl[...])
        pair_g.wait_recv()

        @pl.when(chip > 0)
        def _():
            h, l = split(pg_r[0:modes])
            ysend[...] = (
                pg_r[modes:] + mm(cinc[...], h, l) + mm(exit_own[...], zh[...], zl[...])
            )
            for j in range(chips):
                @pl.when(j < chip)
                def _():
                    exit_to(j).start()

    incb[...] = mm(inc[...], uh[0], ul[0], True) + off_a

    def settle(i, moving):
        following = []
        for k in range(2):
            s = k * half + i
            h, l = split(moving[k])
            adj[s] = rest[s] + mm(state[s] + moving[k], vh[s], vl[s])
            following.append(mm_split(h, l, fh[s], fl[s]))
        return tuple(following)

    lax.fori_loop(0, half, settle, (inc[...], incb[...]), unroll=2)

    def waves(b, carry):
        wg[b] = dot(wave[pl.ds(4 * b, 4)].reshape(4 * cols, modes), basis[...])
        return carry

    lax.fori_loop(0, slabs // 4, waves, 0)

    @pl.when(core == 1)
    def _():
        tiles = zsend[...]
        for k in range(1, groups):
            tile_to(k).wait_recv()
            tiles = tiles + zrecv[k]
        ssend[...] = tiles
        for d in range(n):
            @pl.when(me != d)
            def _():
                share_to(d).start()

        inc[...] = jnp.zeros_like(inc)
        for j in range(chips - 1, 0, -1):
            @pl.when(chip < j)
            def _():
                if j < chips - 1:
                    wait_transfer(j)
                wait_exit(j)
                if j == chips - 1:
                    inc[...] = yrecv[j]
                else:
                    h, l = split(trecv[j])
                    inc[...] = mm(inc[...], h, l) + yrecv[j]

        jsend[...] = exit_own[...] + mm(inc[...], th[...], tl[...])
        joining.start()

    @pl.when(core == 0)
    def _():
        joining.wait_recv()
        inc[...] = jrecv[...]

    incb[...] = adj[half] + mm(inc[...], uh[half], ul[half])

    for b in range(slabs // 4):
        for i in range(4):
            s = 4 * b + i
            entering = incb if s < half else inc
            h, l = split(adj[s] + mm(entering[...], uh[s], ul[s]))
            ahl[b, cols * i : cols * (i + 1)] = h
            ahl[b, cols * (4 + i) : cols * (5 + i)] = l

    def products(slot, peer):
        columns = pl.ds(pl.multiple_of(peer * part, 128), part)
        points = basis[:, columns]
        for b in range(slabs // 4):
            ag = dot(ahl[b], points)
            both = wg[b, :, columns] * (ag[: 4 * cols] + ag[4 * cols :])
            for i in range(4):
                esend[slot, 4 * b + i : 4 * b + i + 1] = jnp.sum(
                    both[cols * i : cols * (i + 1)], axis=0, keepdims=True
                )

    copies = []
    low = 0
    high = groups - 1
    for slot in range(groups - 1):
        above = (high - mine >= mine - low).astype(jnp.int32)
        peer = above * high + (1 - above) * low
        low = low + 1 - above
        high = high - above
        products(slot, peer)
        at = lax.rem(peer + groups - mine, groups)
        copies.append(
            pltpu.make_async_remote_copy(
                src_ref=esend.at[slot], dst_ref=erecv.at[at],
                send_sem=es.at[slot], recv_sem=er.at[at],
                device_id=(peer, me), device_id_type=MESH,
            )
        )
        copies[-1].start()
    products(groups - 1, mine)

    @pl.when(core == 0)
    def _():
        cur[...] = jnp.zeros_like(cur)

    @pl.when(core == 1)
    def _():
        cur[...] = ssend[...]

    for j in range(chips):
        @pl.when(me != 2 * j + 1)
        def _():
            copy_to(ssend, srecv.at[j], ss.at[0], sr.at[j], other).wait_recv()
            cur[...] += srecv[j]

    current = jnp.sum(cur[...])
    factor = (all_slabs * grid * (2.0 / small)) / current
    summed = esend[groups - 1]
    for k in range(1, groups):
        pltpu.make_async_remote_copy(
            src_ref=esend.at[0], dst_ref=erecv.at[k], send_sem=es.at[0], recv_sem=er.at[k],
            device_id=(mine, other), device_id_type=MESH,
        ).wait_recv()
        summed = summed + erecv[k]
    out[...] = summed * factor
    for copy in copies:
        copy.wait_send()

    @pl.when(core == 0)
    def _():
        pair_off.wait_send()
        pair_u.wait_send()
        pair_g.wait_send()

    @pl.when(core == 1)
    def _():
        entry.wait_send()
        joining.wait_send()
        for k in range(1, groups):
            tile_to(k).wait_send()
        for d in range(n):
            @pl.when(me != d)
            def _():
                share_to(d).wait_send()

        @pl.when(onward)
        def _():
            offset_on.wait_send()

        @pl.when(jnp.logical_and(onward, chip > 0))
        def _():
            transfer_on.wait_send()

        @pl.when(jnp.logical_and(odd == 1, chip < chips - 1))
        def _():
            carried_to(0).wait_send()

            @pl.when(chip < chips - 2)
            def _():
                carried_to(1).wait_send()

        @pl.when(inner)
        def _():
            for j in range(chips):
                @pl.when(j < chip)
                def _():
                    transfer_to(j).wait_send()

        @pl.when(chip > 0)
        def _():
            for j in range(chips):
                @pl.when(j < chip)
                def _():
                    exit_to(j).wait_send()


def local(wavefunction, injected_modes, factor_blocks, pivot_inverse, mode_velocity, energy_weight, mode_basis):
    n = lax.axis_size("slab")
    groups = lax.axis_size("energy")
    _, slabs, cols, modes = wavefunction.shape
    grid = mode_basis.shape[1]
    part = grid // groups
    chips = n // 2
    vmem = pl.BlockSpec(memory_space=pltpu.VMEM)
    hbm = pl.BlockSpec(memory_space=pl.ANY)
    dma = pltpu.SemaphoreType.DMA

    def full(*shape):
        return pltpu.VMEM(shape, F32)

    def short(*shape):
        return pltpu.VMEM(shape, BF16)

    result = pl.pallas_call(
        functools.partial(kernel, n, groups),
        out_shape=jax.ShapeDtypeStruct((slabs, part), F32),
        in_specs=[vmem, vmem, hbm, hbm, vmem, vmem, vmem],
        out_specs=vmem,
        scratch_shapes=[
            full(slabs, modes, modes),
            full(slabs, modes, modes),
            short(slabs // 4, 8 * cols, modes),
            dma((slabs,)),
            dma,
        ]
        + [short(slabs, modes, modes)] * 6
        + [short(modes, modes)] * 8
        + [short(2, modes, modes)] * 2
        + [short(slabs, cols, modes)] * 2
        + [full(slabs, cols, modes)] * 3
        + [
            full(slabs // 4, 4 * cols, grid),
            full(2, cols, modes),
        ]
        + [full(cols, modes)] * 5
        + [full(cols, modes)] * 3
        + [full(8, 128)]
        + [full(cols + 8, modes)] * 2
        + [full(modes, modes)] * 2
        + [full(modes + cols, modes)] * 2
        + [full(cols, modes)] * 2
        + [
            full(modes, modes),
            full(chips, modes, modes),
            full(modes, modes),
        ]
        + [full(cols, modes)] * 2
        + [full(cols, modes)] * 2
        + [full(cols, modes), full(chips, cols, modes)]
        + [full(cols, modes)] * 2
        + [full(8, 128), full(groups, 8, 128)]
        + [full(8, 128), full(chips, 8, 128)]
        + [full(groups, slabs, part)] * 2
        + [dma] * 6
        + [dma] * 4
        + [dma((chips,))] * 2
        + [dma((2,)), dma]
        + [dma] * 2
        + [dma((chips,))] * 2
        + [dma] * 2
        + [dma((groups,))] * 2
        + [dma((n,)), dma((chips,))]
        + [dma((groups,))] * 2,
        compiler_params=pltpu.CompilerParams(
            collective_id=0, has_side_effects=True, vmem_limit_bytes=60 * 1024 * 1024
        ),
    )(
        wavefunction[0],
        injected_modes,
        factor_blocks[0],
        pivot_inverse[0],
        mode_velocity,
        energy_weight.reshape(1, 1),
        mode_basis,
    )
    return result.T


def solution(mesh):
    return jax.shard_map(
        local,
        mesh=mesh,
        in_specs=(
            P("energy", "slab", None, None),
            P("energy", None),
            P("energy", "slab", None, None),
            P("energy", "slab", None, None),
            P("energy", None),
            P("energy"),
            P(),
        ),
        out_specs=P("energy", "slab"),
        check_vma=False,
    )
```

```python
import functools
import jax
import jax.numpy as jnp
from jax import lax
from jax.experimental import pallas as pl
from jax.experimental.pallas import tpu as pltpu
from jax.sharding import PartitionSpec as P

F32 = jnp.float32
BF16 = jnp.bfloat16
MESH = pl.DeviceIdType.MESH


def split(x):
    hi = x.astype(BF16)
    return hi, (x - hi.astype(F32)).astype(BF16)


def dot(a, b, transposed=False):
    return lax.dot_general(
        a, b, (((1,), (1 if transposed else 0,)), ((), ())), preferred_element_type=F32
    )


def mm_split(ah, al, bh, bl, transposed=False):
    rows = ah.shape[0]
    both = dot(jnp.concatenate([ah, al], axis=0), bh, transposed)
    return both[:rows] + both[rows:] + dot(ah, bl, transposed)


def mm(a, bh, bl, transposed=False):
    ah, al = split(a)
    return mm_split(ah, al, bh, bl, transposed)


def kernel(
    n, groups,
    wave, inj, fac_hbm, piv_hbm, vel, ew, basis,
    out,
    fac, piv, ahl, fac_sem, piv_sem,
    fh, fl, uh, ul, vh, vl, xh, xl, th, tl, zh, zl, wh, wl, gh, gl, srh, srl,
    rest, adj, wg, off, scaled_ref, whole_off, chip_off, local_e, exit_own,
    inc, incb, cinc, cur,
    po_s, po_r, pu_s, pu_r, pg_s, pg_r, osend, orecv, tsend, trecv, urecv, csend, crecv,
    isend, irecv, ysend, yrecv, jsend, jrecv, zsend, zrecv, ssend, srecv, esend, erecv,
    pos, por, pus, pur, pgs, pgr, os, our, us, ur, ts, tr, cs, cr, is_, ir, ys, yr, js, jr,
    zs, zr, ss, sr, es, er,
):
    me = lax.axis_index("slab")
    mine = lax.axis_index("energy")
    slabs, cols, modes = wave.shape
    grid = basis.shape[1]
    part = grid // groups
    chips = n // 2
    chip = me // 2
    core = lax.rem(me, 2)
    other = me + 1 - 2 * core
    odd = lax.rem(chip, 2)
    half = slabs // 2
    all_slabs = n * slabs
    small = 2.0 / (all_slabs * cols * modes * groups * 4096.0)

    def factor_in(s):
        return pltpu.make_async_copy(fac_hbm.at[s], fac.at[s], fac_sem.at[s])

    for i in range(half):
        for k in range(2):
            factor_in(k * half + half - 1 - i).start()
    pivots_in = pltpu.make_async_copy(piv_hbm, piv, piv_sem)
    pivots_in.start()

    barrier = pltpu.get_barrier_semaphore()

    for k in range(1, n):
        pl.semaphore_signal(
            barrier, inc=1, device_id=(mine, lax.rem(me + k, n)), device_id_type=MESH
        )
    for k in range(1, groups):
        peer = lax.rem(mine + k, groups)
        pl.semaphore_signal(barrier, inc=1, device_id=(peer, me), device_id_type=MESH)

    rows_at = lax.broadcasted_iota(jnp.int32, (cols, cols), 0)
    cols_at = lax.broadcasted_iota(jnp.int32, (cols, cols), 1)
    picked = jnp.sum(
        jnp.where(rows_at == cols_at, jnp.broadcast_to(inj[...].astype(F32), (cols, cols)), 0.0),
        axis=1, keepdims=True,
    )
    mode_at = lax.broadcasted_iota(jnp.int32, (cols, modes), 1).astype(F32)
    velocity = jnp.broadcast_to(vel[...], (cols, modes))
    at_injected = jnp.sum(jnp.where(mode_at == picked, velocity, 0.0), axis=1, keepdims=True)
    scaled_ref[...] = ew[...] * (1.0 / at_injected) * velocity

    cur[...] = jnp.zeros_like(cur)

    def bring(s):
        w = wave[s].astype(F32)
        sw = scaled_ref[...] * w
        sq = sw * w
        part_sum = sq[0:8]
        for j in range(1, cols // 8):
            part_sum = part_sum + sq[8 * j : 8 * j + 8]
        tile = part_sum[:, 0:128]
        for j in range(1, modes // 128):
            tile = tile + part_sum[:, 128 * j : 128 * j + 128]
        cur[...] += tile
        h, l = split(sw * small)
        srh[s] = h
        srl[s] = l
        factor_in(s).wait()
        h, l = split(fac[s])
        fh[s] = h
        fl[s] = l
        return h, l

    for k in range(2):
        end = k * half + half - 1
        h, l = bring(end)
        uh[end] = h
        ul[end] = l
        off[k] = jnp.zeros((cols, modes), F32)

    def extended(s, h, l, bh, bl):
        return mm_split(
            jnp.concatenate([h, srh[s + 1]], axis=0), jnp.concatenate([l, srl[s + 1]], axis=0), bh, bl
        )

    def chain(i, carry):
        blocks = [bring(k * half + half - 2 - i) for k in range(2)]
        moved = []
        for k in range(2):
            s = k * half + half - 2 - i
            h, l = blocks[k]
            moved.append(extended(s, h, l, uh[s + 1], ul[s + 1]))
        for k in range(2):
            s = k * half + half - 2 - i
            h, l = split(moved[k][0:modes])
            uh[s] = h
            ul[s] = l
            off[k] += moved[k][modes:]
        return carry

    def settle_ends():
        pivots_in.wait()
        for k in range(2):
            end = k * half + half - 1
            h, l = split(piv[end])
            vh[end] = h
            vl[end] = l
            rest[end] = jnp.zeros((cols, modes), F32)

    def climb(i, carry):
        firsts = []
        for k in range(2):
            s = k * half + half - 2 - i
            first = extended(s, fh[s], fl[s], vh[s + 1], vl[s + 1])
            firsts.append(jnp.concatenate([first[0:modes], first[modes:] + rest[s + 1]], axis=0))
        seconds = []
        for k in range(2):
            s = k * half + half - 2 - i
            seconds.append(mm(firsts[k], fh[s], fl[s], True))
        for k in range(2):
            s = k * half + half - 2 - i
            h, l = split(piv[s] + seconds[k][0:modes])
            vh[s] = h
            vl[s] = l
            rest[s] = seconds[k][modes:]
        return carry

    beside = (half - 1) // 2 + -1
    for i in range(half - 1):
        chain(i, 0)
        if i == half - 2 - beside:
            settle_ends()
        elif i > half - 2 - beside:
            climb(i - (half - 1 - beside), 0)

    def copy_to(source, target, send, receive, device):
        return pltpu.make_async_remote_copy(
            src_ref=source, dst_ref=target, send_sem=send, recv_sem=receive,
            device_id=(mine, device), device_id_type=MESH,
        )

    pair_off = copy_to(po_s, po_r, pos, por, other)
    pair_u = copy_to(pu_s, pu_r, pus, pur, other)
    pair_g = copy_to(pg_s, pg_r, pgs, pgr, other)
    entry = copy_to(isend, irecv, is_, ir, other)
    joining = copy_to(jsend, jrecv, js, jr, other)

    def chip_at(j):
        return 2 * lax.rem(j, chips) + 1

    offset_on = copy_to(osend, orecv, os, our, chip_at(chip + 1))
    transfer_on = copy_to(tsend, urecv, us, ur, chip_at(chip + 1))

    def carried_to(k):
        return copy_to(csend, crecv, cs.at[k], cr, chip_at(chip + 1 + k))

    def transfer_to(j):
        return copy_to(tsend, trecv.at[chip], ts.at[j], tr.at[chip], 2 * j + 1)

    def exit_to(j):
        return copy_to(ysend, yrecv.at[chip], ys.at[j], yr.at[chip], 2 * j + 1)

    def wait_transfer(j):
        copy_to(tsend, trecv.at[j], ts.at[j], tr.at[j], other).wait_recv()

    def wait_exit(j):
        copy_to(ysend, yrecv.at[j], ys.at[j], yr.at[j], other).wait_recv()

    def tile_to(k):
        peer = lax.rem(mine + k, groups)
        return pltpu.make_async_remote_copy(
            src_ref=zsend, dst_ref=zrecv.at[k], send_sem=zs.at[k], recv_sem=zr.at[k],
            device_id=(peer, me), device_id_type=MESH,
        )

    def share_to(d):
        return copy_to(ssend, srecv.at[chip], ss.at[d], sr.at[chip], d)

    inner = jnp.logical_and(chip > 0, chip < chips - 1)
    onward = jnp.logical_and(odd == 0, chip < chips - 1)

    off[0] += mm_split(srh[0], srl[0], uh[0], ul[0])
    off_a = off[0]
    off_b = off[1] + mm_split(srh[half], srl[half], uh[half], ul[half])
    whole_off[...] = mm(off_a, uh[half], ul[half]) + off_b
    po_s[0:cols] = whole_off[...]
    po_s[cols:, 0:128] = cur[...]
    po_s[cols:, 128:] = jnp.zeros((8, modes - 128), F32)

    pl.semaphore_wait(barrier, n + groups - 2)

    @pl.when(core == 0)
    def _():
        pair_off.start()

    whole = mm_split(uh[0], ul[0], uh[half], ul[half])
    h, l = split(whole)
    th[...] = h
    tl[...] = l

    @pl.when(core == 0)
    def _():
        pu_s[...] = whole
        pair_u.start()

    @pl.when(core == 1)
    def _():
        pair_off.wait_recv()
        chip_off[...] = mm(po_r[0:cols], th[...], tl[...]) + whole_off[...]

        @pl.when(onward)
        def _():
            osend[...] = chip_off[...]
            offset_on.start()

        zsend[...] = cur[...] + po_r[cols:, 0:128]
        for k in range(1, groups):
            tile_to(k).start()
        pair_u.wait_recv()
        h, l = split(pu_r[...])
        zh[...] = h
        zl[...] = l
        joined = mm_split(h, l, th[...], tl[...])
        tsend[...] = joined

        @pl.when(jnp.logical_and(onward, chip > 0))
        def _():
            transfer_on.start()

        h, l = split(joined)
        wh[...] = h
        wl[...] = l

    early = min(beside + 2, half - 1)
    for i in range(beside, early):
        climb(i, 0)

    def carry_on():
        csend[...] = mm(cinc[...], wh[...], wl[...]) + chip_off[...]
        carried_to(0).start()

        @pl.when(chip < chips - 2)
        def _():
            carried_to(1).start()

    cinc[...] = jnp.zeros_like(cinc)

    @pl.when(core == 1)
    def _():
        @pl.when(chip == 1)
        def _():
            offset_on.wait_recv()
            cinc[...] = orecv[...]
            if chips > 2:
                carry_on()

        @pl.when(inner)
        def _():
            for j in range(chips):
                @pl.when(j < chip)
                def _():
                    transfer_to(j).start()

    for i in range(early, half - 1):
        climb(i, 0)

    row_h, row_l = split(srh[half].astype(F32) + srl[half].astype(F32) + off_a)
    first = mm_split(
        jnp.concatenate([uh[0], row_h], axis=0),
        jnp.concatenate([ul[0], row_l], axis=0),
        vh[half], vl[half],
    )
    first = jnp.concatenate([first[0:modes], first[modes:] + rest[half]], axis=0)
    second = mm(first, uh[0], ul[0], True)
    own_g = second[0:modes] + vh[0].astype(F32) + vl[0].astype(F32)
    own_e = second[modes:] + rest[0] + mm_split(srh[0], srl[0], vh[0], vl[0])

    @pl.when(core == 0)
    def _():
        pg_s[0:modes] = own_g
        pg_s[modes:] = own_e
        pair_g.start()
        entry.wait_recv()
        inc[...] = irecv[...]

    @pl.when(core == 1)
    def _():
        h, l = split(own_g)
        gh[...] = h
        gl[...] = l
        local_e[...] = own_e

        @pl.when(chip > 1)
        def _():
            carried_to(0).wait_recv()
            cinc[...] = crecv[...]

            @pl.when(odd == 1)
            def _():
                offset_on.wait_recv()
                transfer_on.wait_recv()
                h, l = split(urecv[...])
                cinc[...] = mm(cinc[...], h, l) + orecv[...]

                @pl.when(chip < chips - 1)
                def _():
                    carry_on()

        isend[...] = cinc[...]
        entry.start()
        inc[...] = mm(cinc[...], zh[...], zl[...]) + po_r[0:cols]
        exit_own[...] = local_e[...] + mm(inc[...], gh[...], gl[...])
        pair_g.wait_recv()

        @pl.when(chip > 0)
        def _():
            h, l = split(pg_r[0:modes])
            ysend[...] = (
                pg_r[modes:] + mm(cinc[...], h, l) + mm(exit_own[...], zh[...], zl[...], True)
            )
            for j in range(chips):
                @pl.when(j < chip)
                def _():
                    exit_to(j).start()

    incb[...] = mm(inc[...], uh[0], ul[0]) + off_a

    def settle(i, moving):
        following = []
        for k in range(2):
            s = k * half + i
            h, l = split(moving[k] + (srh[s].astype(F32) + srl[s].astype(F32)))
            adj[s] = rest[s] + mm_split(h, l, vh[s], vl[s])
            following.append(mm_split(h, l, fh[s], fl[s]))
            xh[s] = uh[s].T
            xl[s] = ul[s].T
        return tuple(following)

    lax.fori_loop(0, half, settle, (inc[...], incb[...]), unroll=2)

    def waves(b, carry):
        wg[b] = dot(wave[pl.ds(4 * b, 4)].reshape(4 * cols, modes), basis[...])
        return carry

    lax.fori_loop(0, slabs // 4, waves, 0)

    @pl.when(core == 1)
    def _():
        tiles = zsend[...]
        for k in range(1, groups):
            tile_to(k).wait_recv()
            tiles = tiles + zrecv[k]
        ssend[...] = tiles
        for d in range(n):
            @pl.when(me != d)
            def _():
                share_to(d).start()

        inc[...] = jnp.zeros_like(inc)
        for j in range(chips - 1, 0, -1):
            @pl.when(chip < j)
            def _():
                if j < chips - 1:
                    wait_transfer(j)
                wait_exit(j)
                if j == chips - 1:
                    inc[...] = yrecv[j]
                else:
                    h, l = split(trecv[j])
                    inc[...] = mm(inc[...], h, l, True) + yrecv[j]

        jsend[...] = exit_own[...] + mm(inc[...], th[...], tl[...], True)
        joining.start()

    @pl.when(core == 0)
    def _():
        joining.wait_recv()
        inc[...] = jrecv[...]

    incb[...] = adj[half] + mm(inc[...], xh[half], xl[half])

    for b in range(slabs // 4):
        for i in range(4):
            s = 4 * b + i
            entering = incb if s < half else inc
            h, l = split(adj[s] + mm(entering[...], xh[s], xl[s]))
            ahl[b, cols * i : cols * (i + 1)] = h
            ahl[b, cols * (4 + i) : cols * (5 + i)] = l

    def products(slot, peer):
        columns = pl.ds(pl.multiple_of(peer * part, 128), part)
        points = basis[:, columns]
        for b in range(slabs // 4):
            ag = dot(ahl[b], points)
            both = wg[b, :, columns] * (ag[: 4 * cols] + ag[4 * cols :])
            for i in range(4):
                esend[slot, 4 * b + i : 4 * b + i + 1] = jnp.sum(
                    both[cols * i : cols * (i + 1)], axis=0, keepdims=True
                )

    copies = []
    low = 0
    high = groups - 1
    for slot in range(groups - 1):
        above = (high - mine >= mine - low).astype(jnp.int32)
        peer = above * high + (1 - above) * low
        low = low + 1 - above
        high = high - above
        products(slot, peer)
        at = lax.rem(peer + groups - mine, groups)
        copies.append(
            pltpu.make_async_remote_copy(
                src_ref=esend.at[slot], dst_ref=erecv.at[at],
                send_sem=es.at[slot], recv_sem=er.at[at],
                device_id=(peer, me), device_id_type=MESH,
            )
        )
        copies[-1].start()
    products(groups - 1, mine)

    @pl.when(core == 0)
    def _():
        cur[...] = jnp.zeros_like(cur)

    @pl.when(core == 1)
    def _():
        cur[...] = ssend[...]

    for j in range(chips):
        @pl.when(me != 2 * j + 1)
        def _():
            copy_to(ssend, srecv.at[j], ss.at[0], sr.at[j], other).wait_recv()
            cur[...] += srecv[j]

    current = jnp.sum(cur[...])
    factor = (all_slabs * grid * (2.0 / small)) / current
    summed = esend[groups - 1]
    for k in range(1, groups):
        pltpu.make_async_remote_copy(
            src_ref=esend.at[0], dst_ref=erecv.at[k], send_sem=es.at[0], recv_sem=er.at[k],
            device_id=(mine, other), device_id_type=MESH,
        ).wait_recv()
        summed = summed + erecv[k]
    out[...] = summed * factor
    for copy in copies:
        copy.wait_send()

    @pl.when(core == 0)
    def _():
        pair_off.wait_send()
        pair_u.wait_send()
        pair_g.wait_send()

    @pl.when(core == 1)
    def _():
        entry.wait_send()
        joining.wait_send()
        for k in range(1, groups):
            tile_to(k).wait_send()
        for d in range(n):
            @pl.when(me != d)
            def _():
                share_to(d).wait_send()

        @pl.when(onward)
        def _():
            offset_on.wait_send()

        @pl.when(jnp.logical_and(onward, chip > 0))
        def _():
            transfer_on.wait_send()

        @pl.when(jnp.logical_and(odd == 1, chip < chips - 1))
        def _():
            carried_to(0).wait_send()

            @pl.when(chip < chips - 2)
            def _():
                carried_to(1).wait_send()

        @pl.when(inner)
        def _():
            for j in range(chips):
                @pl.when(j < chip)
                def _():
                    transfer_to(j).wait_send()

        @pl.when(chip > 0)
        def _():
            for j in range(chips):
                @pl.when(j < chip)
                def _():
                    exit_to(j).wait_send()


def local(wavefunction, injected_modes, factor_blocks, pivot_inverse, mode_velocity, energy_weight, mode_basis):
    n = lax.axis_size("slab")
    groups = lax.axis_size("energy")
    _, slabs, cols, modes = wavefunction.shape
    grid = mode_basis.shape[1]
    part = grid // groups
    chips = n // 2
    vmem = pl.BlockSpec(memory_space=pltpu.VMEM)
    hbm = pl.BlockSpec(memory_space=pl.ANY)
    dma = pltpu.SemaphoreType.DMA

    def full(*shape):
        return pltpu.VMEM(shape, F32)

    def short(*shape):
        return pltpu.VMEM(shape, BF16)

    result = pl.pallas_call(
        functools.partial(kernel, n, groups),
        out_shape=jax.ShapeDtypeStruct((slabs, part), F32),
        in_specs=[vmem, vmem, hbm, hbm, vmem, vmem, vmem],
        out_specs=vmem,
        scratch_shapes=[
            full(slabs, modes, modes),
            full(slabs, modes, modes),
            short(slabs // 4, 8 * cols, modes),
            dma((slabs,)),
            dma,
        ]
        + [short(slabs, modes, modes)] * 8
        + [short(modes, modes)] * 8
        + [short(slabs, cols, modes)] * 2
        + [full(slabs, cols, modes)] * 2
        + [
            full(slabs // 4, 4 * cols, grid),
            full(2, cols, modes),
        ]
        + [full(cols, modes)] * 5
        + [full(cols, modes)] * 3
        + [full(8, 128)]
        + [full(cols + 8, modes)] * 2
        + [full(modes, modes)] * 2
        + [full(modes + cols, modes)] * 2
        + [full(cols, modes)] * 2
        + [
            full(modes, modes),
            full(chips, modes, modes),
            full(modes, modes),
        ]
        + [full(cols, modes)] * 2
        + [full(cols, modes)] * 2
        + [full(cols, modes), full(chips, cols, modes)]
        + [full(cols, modes)] * 2
        + [full(8, 128), full(groups, 8, 128)]
        + [full(8, 128), full(chips, 8, 128)]
        + [full(groups, slabs, part)] * 2
        + [dma] * 6
        + [dma] * 4
        + [dma((chips,))] * 2
        + [dma((2,)), dma]
        + [dma] * 2
        + [dma((chips,))] * 2
        + [dma] * 2
        + [dma((groups,))] * 2
        + [dma((n,)), dma((chips,))]
        + [dma((groups,))] * 2,
        compiler_params=pltpu.CompilerParams(
            collective_id=0, has_side_effects=True, vmem_limit_bytes=60 * 1024 * 1024
        ),
    )(
        wavefunction[0],
        injected_modes,
        factor_blocks[0],
        pivot_inverse[0],
        mode_velocity,
        energy_weight.reshape(1, 1),
        mode_basis,
    )
    return result.T


def solution(mesh):
    return jax.shard_map(
        local,
        mesh=mesh,
        in_specs=(
            P("energy", "slab", None, None),
            P("energy", None),
            P("energy", "slab", None, None),
            P("energy", "slab", None, None),
            P("energy", None),
            P("energy"),
            P(),
        ),
        out_specs=P("energy", "slab"),
        check_vma=False,
    )
```

```python
import functools
import jax
import jax.numpy as jnp
from jax import lax
from jax.experimental import pallas as pl
from jax.experimental.pallas import tpu as pltpu
from jax.sharding import PartitionSpec as P

F32 = jnp.float32
BF16 = jnp.bfloat16
MESH = pl.DeviceIdType.MESH


def split(x):
    hi = x.astype(BF16)
    return hi, (x - hi.astype(F32)).astype(BF16)


def dot(a, b, transposed=False):
    return lax.dot_general(
        a, b, (((1,), (1 if transposed else 0,)), ((), ())), preferred_element_type=F32
    )


def mm_split(ah, al, bh, bl, transposed=False):
    rows = ah.shape[0]
    both = dot(jnp.concatenate([ah, al], axis=0), bh, transposed)
    return both[:rows] + both[rows:] + dot(ah, bl, transposed)


def mm(a, bh, bl, transposed=False):
    ah, al = split(a)
    return mm_split(ah, al, bh, bl, transposed)


def kernel(
    n, groups,
    wave, inj, fac_hbm, piv_hbm, vel, ew, basis,
    out,
    fac, piv, ahl, fac_sem, piv_sem,
    fh, fl, uh, ul, vh, vl, xh, xl, th, tl, zh, zl, wh, wl, gh, gl, srh, srl,
    rest, adj, wg, off, scaled_ref, whole_off, chip_off, local_e, exit_own,
    inc, incb, cinc, cur,
    po_s, po_r, pu_s, pu_r, pg_s, pg_r, osend, orecv, tsend, trecv, urecv, csend, crecv,
    isend, irecv, ysend, yrecv, jsend, jrecv, zsend, zrecv, ssend, srecv, esend, erecv,
    pos, por, pus, pur, pgs, pgr, os, our, us, ur, ts, tr, cs, cr, is_, ir, ys, yr, js, jr,
    zs, zr, ss, sr, es, er,
):
    me = lax.axis_index("slab")
    mine = lax.axis_index("energy")
    slabs, cols, modes = wave.shape
    grid = basis.shape[1]
    part = grid // groups
    chips = n // 2
    chip = me // 2
    core = lax.rem(me, 2)
    other = me + 1 - 2 * core
    odd = lax.rem(chip, 2)
    half = slabs // 2
    all_slabs = n * slabs
    small = 2.0 / (all_slabs * cols * modes * groups * 4096.0)

    starts = {}
    top = half
    for size in (1, 1, 2, slabs):
        size = min(size, top)
        if size:
            starts[top - 1] = pltpu.make_async_copy(
                fac_hbm.at[:, top - size : top], fac.at[:, top - size : top], fac_sem.at[len(starts)]
            )
            starts[top - 1].start()
            top = top - size
    pivots_in = pltpu.make_async_copy(piv_hbm, piv, piv_sem)
    pivots_in.start()

    barrier = pltpu.get_barrier_semaphore()

    for k in range(1, n):
        pl.semaphore_signal(
            barrier, inc=1, device_id=(mine, lax.rem(me + k, n)), device_id_type=MESH
        )
    for k in range(1, groups):
        peer = lax.rem(mine + k, groups)
        pl.semaphore_signal(barrier, inc=1, device_id=(peer, me), device_id_type=MESH)

    rows_at = lax.broadcasted_iota(jnp.int32, (cols, cols), 0)
    cols_at = lax.broadcasted_iota(jnp.int32, (cols, cols), 1)
    picked = jnp.sum(
        jnp.where(rows_at == cols_at, jnp.broadcast_to(inj[...].astype(F32), (cols, cols)), 0.0),
        axis=1, keepdims=True,
    )
    mode_at = lax.broadcasted_iota(jnp.int32, (cols, modes), 1).astype(F32)
    velocity = jnp.broadcast_to(vel[...], (cols, modes))
    at_injected = jnp.sum(jnp.where(mode_at == picked, velocity, 0.0), axis=1, keepdims=True)
    scaled_ref[...] = ew[...] * (1.0 / at_injected) * velocity

    cur[...] = jnp.zeros_like(cur)

    def bring(k, i):
        s = k * half + i
        w = wave[s].astype(F32)
        sw = scaled_ref[...] * w
        sq = sw * w
        part_sum = sq[0:8]
        for j in range(1, cols // 8):
            part_sum = part_sum + sq[8 * j : 8 * j + 8]
        tile = part_sum[:, 0:128]
        for j in range(1, modes // 128):
            tile = tile + part_sum[:, 128 * j : 128 * j + 128]
        cur[...] += tile
        h, l = split(sw * small)
        srh[s] = h
        srl[s] = l
        h, l = split(fac[k, i])
        fh[s] = h
        fl[s] = l
        return h, l

    starts[half - 1].wait()
    for k in range(2):
        end = k * half + half - 1
        h, l = bring(k, half - 1)
        uh[end] = h
        ul[end] = l
        off[k] = jnp.zeros((cols, modes), F32)

    def extended(s, h, l, bh, bl):
        return mm_split(
            jnp.concatenate([h, srh[s + 1]], axis=0), jnp.concatenate([l, srl[s + 1]], axis=0), bh, bl
        )

    def chain(i, carry):
        if half - 2 - i in starts:
            starts[half - 2 - i].wait()
        blocks = [bring(k, half - 2 - i) for k in range(2)]
        moved = []
        for k in range(2):
            s = k * half + half - 2 - i
            h, l = blocks[k]
            moved.append(extended(s, h, l, uh[s + 1], ul[s + 1]))
        for k in range(2):
            s = k * half + half - 2 - i
            h, l = split(moved[k][0:modes])
            uh[s] = h
            ul[s] = l
            off[k] += moved[k][modes:]
        return carry

    def settle_ends():
        pivots_in.wait()
        for k in range(2):
            end = k * half + half - 1
            h, l = split(piv[end])
            vh[end] = h
            vl[end] = l
            rest[end] = jnp.zeros((cols, modes), F32)

    def climb(i, carry):
        firsts = []
        for k in range(2):
            s = k * half + half - 2 - i
            first = extended(s, fh[s], fl[s], vh[s + 1], vl[s + 1])
            firsts.append(jnp.concatenate([first[0:modes], first[modes:] + rest[s + 1]], axis=0))
        seconds = []
        for k in range(2):
            s = k * half + half - 2 - i
            seconds.append(mm(firsts[k], fh[s], fl[s], True))
        for k in range(2):
            s = k * half + half - 2 - i
            h, l = split(piv[s] + seconds[k][0:modes])
            vh[s] = h
            vl[s] = l
            rest[s] = seconds[k][modes:]
        return carry

    beside = (half - 1) // 2 + -1
    for i in range(half - 1):
        chain(i, 0)
        if i == half - 2 - beside:
            settle_ends()
        elif i > half - 2 - beside:
            climb(i - (half - 1 - beside), 0)

    def copy_to(source, target, send, receive, device):
        return pltpu.make_async_remote_copy(
            src_ref=source, dst_ref=target, send_sem=send, recv_sem=receive,
            device_id=(mine, device), device_id_type=MESH,
        )

    pair_off = copy_to(po_s, po_r, pos, por, other)
    pair_u = copy_to(pu_s, pu_r, pus, pur, other)
    pair_g = copy_to(pg_s, pg_r, pgs, pgr, other)
    entry = copy_to(isend, irecv, is_, ir, other)
    joining = copy_to(jsend, jrecv, js, jr, other)

    def chip_at(j):
        return 2 * lax.rem(j, chips) + 1

    offset_on = copy_to(osend, orecv, os, our, chip_at(chip + 1))
    transfer_on = copy_to(tsend, urecv, us, ur, chip_at(chip + 1))

    def carried_to(k):
        return copy_to(csend, crecv, cs.at[k], cr, chip_at(chip + 1 + k))

    def transfer_to(j):
        return copy_to(tsend, trecv.at[chip], ts.at[j], tr.at[chip], 2 * j + 1)

    def exit_to(j):
        return copy_to(ysend, yrecv.at[chip], ys.at[j], yr.at[chip], 2 * j + 1)

    def wait_transfer(j):
        copy_to(tsend, trecv.at[j], ts.at[j], tr.at[j], other).wait_recv()

    def wait_exit(j):
        copy_to(ysend, yrecv.at[j], ys.at[j], yr.at[j], other).wait_recv()

    def tile_to(k):
        peer = lax.rem(mine + k, groups)
        return pltpu.make_async_remote_copy(
            src_ref=zsend, dst_ref=zrecv.at[k], send_sem=zs.at[k], recv_sem=zr.at[k],
            device_id=(peer, me), device_id_type=MESH,
        )

    def share_to(d):
        return copy_to(ssend, srecv.at[chip], ss.at[d], sr.at[chip], d)

    inner = jnp.logical_and(chip > 0, chip < chips - 1)
    onward = jnp.logical_and(odd == 0, chip < chips - 1)

    off[0] += mm_split(srh[0], srl[0], uh[0], ul[0])
    off_a = off[0]
    off_b = off[1] + mm_split(srh[half], srl[half], uh[half], ul[half])
    whole_off[...] = mm(off_a, uh[half], ul[half]) + off_b
    po_s[0:cols] = whole_off[...]
    po_s[cols:, 0:128] = cur[...]
    po_s[cols:, 128:] = jnp.zeros((8, modes - 128), F32)

    pl.semaphore_wait(barrier, n + groups - 2)

    @pl.when(core == 0)
    def _():
        pair_off.start()

    whole = mm_split(uh[0], ul[0], uh[half], ul[half])
    h, l = split(whole)
    th[...] = h
    tl[...] = l

    @pl.when(core == 0)
    def _():
        pu_s[...] = whole
        pair_u.start()

    @pl.when(core == 1)
    def _():
        pair_off.wait_recv()
        chip_off[...] = mm(po_r[0:cols], th[...], tl[...]) + whole_off[...]

        @pl.when(onward)
        def _():
            osend[...] = chip_off[...]
            offset_on.start()

        zsend[...] = cur[...] + po_r[cols:, 0:128]
        for k in range(1, groups):
            tile_to(k).start()
        pair_u.wait_recv()
        h, l = split(pu_r[...])
        zh[...] = h
        zl[...] = l
        joined = mm_split(h, l, th[...], tl[...])
        tsend[...] = joined

        @pl.when(jnp.logical_and(onward, chip > 0))
        def _():
            transfer_on.start()

        h, l = split(joined)
        wh[...] = h
        wl[...] = l

    early = min(beside + 2, half - 1)
    for i in range(beside, early):
        climb(i, 0)

    def carry_on():
        csend[...] = mm(cinc[...], wh[...], wl[...]) + chip_off[...]
        carried_to(0).start()

        @pl.when(chip < chips - 2)
        def _():
            carried_to(1).start()

    cinc[...] = jnp.zeros_like(cinc)

    @pl.when(core == 1)
    def _():
        @pl.when(chip == 1)
        def _():
            offset_on.wait_recv()
            cinc[...] = orecv[...]
            if chips > 2:
                carry_on()

        @pl.when(inner)
        def _():
            for j in range(chips):
                @pl.when(j < chip)
                def _():
                    transfer_to(j).start()

    for i in range(early, half - 1):
        climb(i, 0)

    row_h, row_l = split(srh[half].astype(F32) + srl[half].astype(F32) + off_a)
    first = mm_split(
        jnp.concatenate([uh[0], row_h], axis=0),
        jnp.concatenate([ul[0], row_l], axis=0),
        vh[half], vl[half],
    )
    first = jnp.concatenate([first[0:modes], first[modes:] + rest[half]], axis=0)
    second = mm(first, uh[0], ul[0], True)
    own_g = second[0:modes] + vh[0].astype(F32) + vl[0].astype(F32)
    own_e = second[modes:] + rest[0] + mm_split(srh[0], srl[0], vh[0], vl[0])

    @pl.when(core == 0)
    def _():
        pg_s[0:modes] = own_g
        pg_s[modes:] = own_e
        pair_g.start()
        entry.wait_recv()
        inc[...] = irecv[...]

    @pl.when(core == 1)
    def _():
        h, l = split(own_g)
        gh[...] = h
        gl[...] = l
        local_e[...] = own_e

        @pl.when(chip > 1)
        def _():
            carried_to(0).wait_recv()
            cinc[...] = crecv[...]

            @pl.when(odd == 1)
            def _():
                offset_on.wait_recv()
                transfer_on.wait_recv()
                h, l = split(urecv[...])
                cinc[...] = mm(cinc[...], h, l) + orecv[...]

                @pl.when(chip < chips - 1)
                def _():
                    carry_on()

        isend[...] = cinc[...]
        entry.start()
        inc[...] = mm(cinc[...], zh[...], zl[...]) + po_r[0:cols]
        exit_own[...] = local_e[...] + mm(inc[...], gh[...], gl[...])
        pair_g.wait_recv()

        @pl.when(chip > 0)
        def _():
            h, l = split(pg_r[0:modes])
            ysend[...] = (
                pg_r[modes:] + mm(cinc[...], h, l) + mm(exit_own[...], zh[...], zl[...], True)
            )
            for j in range(chips):
                @pl.when(j < chip)
                def _():
                    exit_to(j).start()

    incb[...] = mm(inc[...], uh[0], ul[0]) + off_a

    def settle(i, moving):
        following = []
        for k in range(2):
            s = k * half + i
            h, l = split(moving[k] + (srh[s].astype(F32) + srl[s].astype(F32)))
            adj[s] = rest[s] + mm_split(h, l, vh[s], vl[s])
            following.append(mm_split(h, l, fh[s], fl[s]))
            xh[s] = uh[s].T
            xl[s] = ul[s].T
        return tuple(following)

    lax.fori_loop(0, half, settle, (inc[...], incb[...]), unroll=2)

    def waves(b, carry):
        wg[b] = dot(wave[pl.ds(4 * b, 4)].reshape(4 * cols, modes), basis[...])
        return carry

    lax.fori_loop(0, slabs // 4, waves, 0)

    @pl.when(core == 1)
    def _():
        tiles = zsend[...]
        for k in range(1, groups):
            tile_to(k).wait_recv()
            tiles = tiles + zrecv[k]
        ssend[...] = tiles
        for d in range(n):
            @pl.when(me != d)
            def _():
                share_to(d).start()

        inc[...] = jnp.zeros_like(inc)
        for j in range(chips - 1, 0, -1):
            @pl.when(chip < j)
            def _():
                if j < chips - 1:
                    wait_transfer(j)
                wait_exit(j)
                if j == chips - 1:
                    inc[...] = yrecv[j]
                else:
                    h, l = split(trecv[j])
                    inc[...] = mm(inc[...], h, l, True) + yrecv[j]

        jsend[...] = exit_own[...] + mm(inc[...], th[...], tl[...], True)
        joining.start()

    @pl.when(core == 0)
    def _():
        joining.wait_recv()
        inc[...] = jrecv[...]

    incb[...] = adj[half] + mm(inc[...], xh[half], xl[half])

    for b in range(slabs // 4):
        for i in range(4):
            s = 4 * b + i
            entering = incb if s < half else inc
            h, l = split(adj[s] + mm(entering[...], xh[s], xl[s]))
            ahl[b, cols * i : cols * (i + 1)] = h
            ahl[b, cols * (4 + i) : cols * (5 + i)] = l

    def products(slot, peer):
        columns = pl.ds(pl.multiple_of(peer * part, 128), part)
        points = basis[:, columns]
        for b in range(slabs // 4):
            ag = dot(ahl[b], points)
            both = wg[b, :, columns] * (ag[: 4 * cols] + ag[4 * cols :])
            for i in range(4):
                esend[slot, 4 * b + i : 4 * b + i + 1] = jnp.sum(
                    both[cols * i : cols * (i + 1)], axis=0, keepdims=True
                )

    copies = []
    low = 0
    high = groups - 1
    for slot in range(groups - 1):
        above = (high - mine >= mine - low).astype(jnp.int32)
        peer = above * high + (1 - above) * low
        low = low + 1 - above
        high = high - above
        products(slot, peer)
        at = lax.rem(peer + groups - mine, groups)
        copies.append(
            pltpu.make_async_remote_copy(
                src_ref=esend.at[slot], dst_ref=erecv.at[at],
                send_sem=es.at[slot], recv_sem=er.at[at],
                device_id=(peer, me), device_id_type=MESH,
            )
        )
        copies[-1].start()
    products(groups - 1, mine)

    @pl.when(core == 0)
    def _():
        cur[...] = jnp.zeros_like(cur)

    @pl.when(core == 1)
    def _():
        cur[...] = ssend[...]

    for j in range(chips):
        @pl.when(me != 2 * j + 1)
        def _():
            copy_to(ssend, srecv.at[j], ss.at[0], sr.at[j], other).wait_recv()
            cur[...] += srecv[j]

    current = jnp.sum(cur[...])
    factor = (all_slabs * grid * (2.0 / small)) / current
    summed = esend[groups - 1]
    for k in range(1, groups):
        pltpu.make_async_remote_copy(
            src_ref=esend.at[0], dst_ref=erecv.at[k], send_sem=es.at[0], recv_sem=er.at[k],
            device_id=(mine, other), device_id_type=MESH,
        ).wait_recv()
        summed = summed + erecv[k]
    out[...] = summed * factor
    for copy in copies:
        copy.wait_send()

    @pl.when(core == 0)
    def _():
        pair_off.wait_send()
        pair_u.wait_send()
        pair_g.wait_send()

    @pl.when(core == 1)
    def _():
        entry.wait_send()
        joining.wait_send()
        for k in range(1, groups):
            tile_to(k).wait_send()
        for d in range(n):
            @pl.when(me != d)
            def _():
                share_to(d).wait_send()

        @pl.when(onward)
        def _():
            offset_on.wait_send()

        @pl.when(jnp.logical_and(onward, chip > 0))
        def _():
            transfer_on.wait_send()

        @pl.when(jnp.logical_and(odd == 1, chip < chips - 1))
        def _():
            carried_to(0).wait_send()

            @pl.when(chip < chips - 2)
            def _():
                carried_to(1).wait_send()

        @pl.when(inner)
        def _():
            for j in range(chips):
                @pl.when(j < chip)
                def _():
                    transfer_to(j).wait_send()

        @pl.when(chip > 0)
        def _():
            for j in range(chips):
                @pl.when(j < chip)
                def _():
                    exit_to(j).wait_send()


def local(wavefunction, injected_modes, factor_blocks, pivot_inverse, mode_velocity, energy_weight, mode_basis):
    n = lax.axis_size("slab")
    groups = lax.axis_size("energy")
    _, slabs, cols, modes = wavefunction.shape
    grid = mode_basis.shape[1]
    part = grid // groups
    chips = n // 2
    vmem = pl.BlockSpec(memory_space=pltpu.VMEM)
    hbm = pl.BlockSpec(memory_space=pl.ANY)
    dma = pltpu.SemaphoreType.DMA

    def full(*shape):
        return pltpu.VMEM(shape, F32)

    def short(*shape):
        return pltpu.VMEM(shape, BF16)

    result = pl.pallas_call(
        functools.partial(kernel, n, groups),
        out_shape=jax.ShapeDtypeStruct((slabs, part), F32),
        in_specs=[vmem, vmem, hbm, hbm, vmem, vmem, vmem],
        out_specs=vmem,
        scratch_shapes=[
            full(2, slabs // 2, modes, modes),
            full(slabs, modes, modes),
            short(slabs // 4, 8 * cols, modes),
            dma((slabs,)),
            dma,
        ]
        + [short(slabs, modes, modes)] * 8
        + [short(modes, modes)] * 8
        + [short(slabs, cols, modes)] * 2
        + [full(slabs, cols, modes)] * 2
        + [
            full(slabs // 4, 4 * cols, grid),
            full(2, cols, modes),
        ]
        + [full(cols, modes)] * 5
        + [full(cols, modes)] * 3
        + [full(8, 128)]
        + [full(cols + 8, modes)] * 2
        + [full(modes, modes)] * 2
        + [full(modes + cols, modes)] * 2
        + [full(cols, modes)] * 2
        + [
            full(modes, modes),
            full(chips, modes, modes),
            full(modes, modes),
        ]
        + [full(cols, modes)] * 2
        + [full(cols, modes)] * 2
        + [full(cols, modes), full(chips, cols, modes)]
        + [full(cols, modes)] * 2
        + [full(8, 128), full(groups, 8, 128)]
        + [full(8, 128), full(chips, 8, 128)]
        + [full(groups, slabs, part)] * 2
        + [dma] * 6
        + [dma] * 4
        + [dma((chips,))] * 2
        + [dma((2,)), dma]
        + [dma] * 2
        + [dma((chips,))] * 2
        + [dma] * 2
        + [dma((groups,))] * 2
        + [dma((n,)), dma((chips,))]
        + [dma((groups,))] * 2,
        compiler_params=pltpu.CompilerParams(
            collective_id=0, has_side_effects=True, vmem_limit_bytes=60 * 1024 * 1024
        ),
    )(
        wavefunction[0],
        injected_modes,
        factor_blocks.reshape(2, slabs // 2, modes, modes),
        pivot_inverse[0],
        mode_velocity,
        energy_weight.reshape(1, 1),
        mode_basis,
    )
    return result.T


def solution(mesh):
    return jax.shard_map(
        local,
        mesh=mesh,
        in_specs=(
            P("energy", "slab", None, None),
            P("energy", None),
            P("energy", "slab", None, None),
            P("energy", "slab", None, None),
            P("energy", None),
            P("energy"),
            P(),
        ),
        out_specs=P("energy", "slab"),
        check_vma=False,
    )
```

```python
import functools
import jax
import jax.numpy as jnp
from jax import lax
from jax.experimental import pallas as pl
from jax.experimental.pallas import tpu as pltpu
from jax.sharding import PartitionSpec as P

F32 = jnp.float32
BF16 = jnp.bfloat16
MESH = pl.DeviceIdType.MESH


def split(x):
    hi = x.astype(BF16)
    return hi, (x - hi.astype(F32)).astype(BF16)


def dot(a, b, transposed=False):
    return lax.dot_general(
        a, b, (((1,), (1 if transposed else 0,)), ((), ())), preferred_element_type=F32
    )


def mm_split(ah, al, bh, bl, transposed=False):
    rows = ah.shape[0]
    both = dot(jnp.concatenate([ah, al], axis=0), bh, transposed)
    return both[:rows] + both[rows:] + dot(ah, bl, transposed)


def mm(a, bh, bl, transposed=False):
    ah, al = split(a)
    return mm_split(ah, al, bh, bl, transposed)


def kernel(
    n, groups,
    wave, inj, fac_hbm, piv_hbm, vel, ew, basis,
    out,
    fac, piv, ahl, fac_sem, piv_sem,
    fh, fl, uh, ul, vh, vl, xh, xl, th, tl, zh, zl, wh, wl, gh, gl, kh, kl, qh, ql, bh, bl, srh, srl,
    rest, adj, wg, off, scaled_ref, whole_off, chip_off, local_e, exit_own,
    inc, incb, cinc, cur,
    po_s, po_r, pu_s, pu_r, pg_s, pg_r, osend, orecv, tsend, trecv, urecv, csend, crecv,
    isend, irecv, ysend, yrecv, jsend, jrecv, zsend, zrecv, ssend, srecv, esend, erecv,
    pos, por, pus, pur, pgs, pgr, os, our, us, ur, ts, tr, cs, cr, is_, ir, ys, yr, js, jr,
    zs, zr, ss, sr, es, er,
):
    me = lax.axis_index("slab")
    mine = lax.axis_index("energy")
    slabs, cols, modes = wave.shape
    grid = basis.shape[1]
    part = grid // groups
    chips = n // 2
    chip = me // 2
    core = lax.rem(me, 2)
    other = me + 1 - 2 * core
    odd = lax.rem(chip, 2)
    half = slabs // 2
    all_slabs = n * slabs
    small = 2.0 / (all_slabs * cols * modes * groups * 4096.0)

    starts = {}
    top = half
    for size in (1, 1, 2, slabs):
        size = min(size, top)
        if size:
            starts[top - 1] = pltpu.make_async_copy(
                fac_hbm.at[:, top - size : top], fac.at[:, top - size : top], fac_sem.at[len(starts)]
            )
            starts[top - 1].start()
            top = top - size
    pivots_in = pltpu.make_async_copy(piv_hbm, piv, piv_sem)
    pivots_in.start()

    barrier = pltpu.get_barrier_semaphore()

    for k in range(1, n):
        pl.semaphore_signal(
            barrier, inc=1, device_id=(mine, lax.rem(me + k, n)), device_id_type=MESH
        )
    for k in range(1, groups):
        peer = lax.rem(mine + k, groups)
        pl.semaphore_signal(barrier, inc=1, device_id=(peer, me), device_id_type=MESH)

    rows_at = lax.broadcasted_iota(jnp.int32, (cols, cols), 0)
    cols_at = lax.broadcasted_iota(jnp.int32, (cols, cols), 1)
    picked = jnp.sum(
        jnp.where(rows_at == cols_at, jnp.broadcast_to(inj[...].astype(F32), (cols, cols)), 0.0),
        axis=1, keepdims=True,
    )
    mode_at = lax.broadcasted_iota(jnp.int32, (cols, modes), 1).astype(F32)
    velocity = jnp.broadcast_to(vel[...], (cols, modes))
    at_injected = jnp.sum(jnp.where(mode_at == picked, velocity, 0.0), axis=1, keepdims=True)
    scaled_ref[...] = ew[...] * (1.0 / at_injected) * velocity

    cur[...] = jnp.zeros_like(cur)

    def bring(k, i):
        s = k * half + i
        w = wave[s].astype(F32)
        sw = scaled_ref[...] * w
        sq = sw * w
        part_sum = sq[0:8]
        for j in range(1, cols // 8):
            part_sum = part_sum + sq[8 * j : 8 * j + 8]
        tile = part_sum[:, 0:128]
        for j in range(1, modes // 128):
            tile = tile + part_sum[:, 128 * j : 128 * j + 128]
        cur[...] += tile
        h, l = split(sw * small)
        srh[s] = h
        srl[s] = l
        h, l = split(fac[k, i])
        fh[s] = h
        fl[s] = l
        return h, l

    starts[half - 1].wait()
    for k in range(2):
        end = k * half + half - 1
        h, l = bring(k, half - 1)
        uh[end] = h
        ul[end] = l
        off[k] = jnp.zeros((cols, modes), F32)

    def extended(s, h, l, bh, bl):
        return mm_split(
            jnp.concatenate([h, srh[s + 1]], axis=0), jnp.concatenate([l, srl[s + 1]], axis=0), bh, bl
        )

    def chain(i, carry):
        if half - 2 - i in starts:
            starts[half - 2 - i].wait()
        blocks = [bring(k, half - 2 - i) for k in range(2)]
        moved = []
        for k in range(2):
            s = k * half + half - 2 - i
            h, l = blocks[k]
            moved.append(extended(s, h, l, uh[s + 1], ul[s + 1]))
        for k in range(2):
            s = k * half + half - 2 - i
            h, l = split(moved[k][0:modes])
            uh[s] = h
            ul[s] = l
            off[k] += moved[k][modes:]
        return carry

    def settle_ends():
        pivots_in.wait()
        for k in range(2):
            end = k * half + half - 1
            h, l = split(piv[end])
            vh[end] = h
            vl[end] = l
            rest[end] = jnp.zeros((cols, modes), F32)

    def lower(k, i):
        s = k * half + half - 2 - i
        first = extended(s, fh[s], fl[s], vh[s + 1], vl[s + 1])
        return s, jnp.concatenate([first[0:modes], first[modes:] + rest[s + 1]], axis=0)

    def place(s, second):
        value = piv[s] + second[0:modes]
        h, l = split(value)
        vh[s] = h
        vl[s] = l
        rest[s] = second[modes:]
        return value

    def climb(i):
        firsts = [lower(1, i)]
        if i > 0:
            firsts.append(lower(0, i - 1))
        seconds = [mm(first, fh[s], fl[s], True) for s, first in firsts]
        for (s, first), second in zip(firsts, seconds):
            place(s, second)

    beside = 2
    for i in range(half - 1):
        chain(i, 0)
        if i == half - 2 - beside:
            settle_ends()
        elif i > half - 2 - beside:
            climb(i - (half - 1 - beside))

    def copy_to(source, target, send, receive, device):
        return pltpu.make_async_remote_copy(
            src_ref=source, dst_ref=target, send_sem=send, recv_sem=receive,
            device_id=(mine, device), device_id_type=MESH,
        )

    pair_off = copy_to(po_s, po_r, pos, por, other)
    pair_u = copy_to(pu_s, pu_r, pus, pur, other)
    pair_g = copy_to(pg_s, pg_r, pgs, pgr, other)
    entry = copy_to(isend, irecv, is_, ir, other)
    joining = copy_to(jsend, jrecv, js, jr, other)

    def chip_at(j):
        return 2 * lax.rem(j, chips) + 1

    offset_on = copy_to(osend, orecv, os, our, chip_at(chip + 1))
    transfer_on = copy_to(tsend, urecv, us, ur, chip_at(chip + 1))

    def carried_to(k):
        return copy_to(csend, crecv, cs.at[k], cr, chip_at(chip + 1 + k))

    def transfer_to(j):
        return copy_to(tsend, trecv.at[chip], ts.at[j], tr.at[chip], 2 * j + 1)

    def exit_to(j):
        return copy_to(ysend, yrecv.at[chip], ys.at[j], yr.at[chip], 2 * j + 1)

    def wait_transfer(j):
        copy_to(tsend, trecv.at[j], ts.at[j], tr.at[j], other).wait_recv()

    def wait_exit(j):
        copy_to(ysend, yrecv.at[j], ys.at[j], yr.at[j], other).wait_recv()

    def tile_to(k):
        peer = lax.rem(mine + k, groups)
        return pltpu.make_async_remote_copy(
            src_ref=zsend, dst_ref=zrecv.at[k], send_sem=zs.at[k], recv_sem=zr.at[k],
            device_id=(peer, me), device_id_type=MESH,
        )

    def share_to(d):
        return copy_to(ssend, srecv.at[chip], ss.at[d], sr.at[chip], d)

    inner = jnp.logical_and(chip > 0, chip < chips - 1)
    onward = jnp.logical_and(odd == 0, chip < chips - 1)

    off[0] += mm_split(srh[0], srl[0], uh[0], ul[0])
    off_a = off[0]
    off_b = off[1] + mm_split(srh[half], srl[half], uh[half], ul[half])
    whole_off[...] = mm(off_a, uh[half], ul[half]) + off_b
    po_s[0:cols] = whole_off[...]
    po_s[cols:, 0:128] = cur[...]
    po_s[cols:, 128:] = jnp.zeros((8, modes - 128), F32)

    pl.semaphore_wait(barrier, n + groups - 2)

    @pl.when(core == 0)
    def _():
        pair_off.start()

    whole = mm_split(uh[0], ul[0], uh[half], ul[half])
    h, l = split(whole)
    th[...] = h
    tl[...] = l

    @pl.when(core == 0)
    def _():
        pu_s[...] = whole
        pair_u.start()

    @pl.when(core == 1)
    def _():
        pair_off.wait_recv()
        chip_off[...] = mm(po_r[0:cols], th[...], tl[...]) + whole_off[...]

        @pl.when(onward)
        def _():
            osend[...] = chip_off[...]
            offset_on.start()

        zsend[...] = cur[...] + po_r[cols:, 0:128]
        for k in range(1, groups):
            tile_to(k).start()
        pair_u.wait_recv()
        h, l = split(pu_r[...])
        zh[...] = h
        zl[...] = l
        joined = mm_split(h, l, th[...], tl[...])
        tsend[...] = joined

        @pl.when(jnp.logical_and(onward, chip > 0))
        def _():
            transfer_on.start()

        h, l = split(joined)
        wh[...] = h
        wl[...] = l

    early = min(beside + 1, half - 1)
    for i in range(beside, early):
        climb(i)

    def carry_on():
        csend[...] = mm(cinc[...], wh[...], wl[...]) + chip_off[...]

        @pl.when(chip < chips - 2)
        def _():
            carried_to(1).start()

        carried_to(0).start()

    cinc[...] = jnp.zeros_like(cinc)

    @pl.when(core == 1)
    def _():
        @pl.when(chip == 1)
        def _():
            offset_on.wait_recv()
            cinc[...] = orecv[...]
            if chips > 2:
                carry_on()

        @pl.when(inner)
        def _():
            for j in range(chips):
                @pl.when(j < chip)
                def _():
                    transfer_to(j).start()

    for i in range(early, half - 1):
        climb(i)

    row_h, row_l = split(srh[half].astype(F32) + srl[half].astype(F32) + off_a)
    joint = mm_split(
        jnp.concatenate([uh[0], row_h], axis=0),
        jnp.concatenate([ul[0], row_l], axis=0),
        vh[half], vl[half],
    )
    joint = jnp.concatenate([joint[0:modes], joint[modes:] + rest[half]], axis=0)
    _, first = lower(0, half - 2)
    second = mm(first, fh[0], fl[0], True)
    joint = mm(joint, uh[0], ul[0], True)
    own_g = joint[0:modes] + place(0, second)
    own_e = joint[modes:] + rest[0] + mm_split(srh[0], srl[0], vh[0], vl[0])

    @pl.when(core == 0)
    def _():
        pg_s[0:modes] = own_g
        pg_s[modes:] = own_e
        pair_g.start()
        entry.wait_recv()
        inc[...] = irecv[...]

    @pl.when(core == 1)
    def _():
        h, l = split(own_g)
        gh[...] = h
        gl[...] = l
        local_e[...] = own_e
        pair_g.wait_recv()
        h, l = split(pg_r[0:modes])
        kh[...] = h
        kl[...] = l

        @pl.when(chip > 1)
        def _():
            @pl.when(odd == 1)
            def _():
                offset_on.wait_recv()
                transfer_on.wait_recv()
                h, l = split(urecv[...])
                qh[...] = h
                ql[...] = l

            carried_to(0).wait_recv()
            cinc[...] = crecv[...]

            @pl.when(odd == 1)
            def _():
                cinc[...] = mm(cinc[...], qh[...], ql[...]) + orecv[...]

                @pl.when(chip < chips - 1)
                def _():
                    carry_on()

        isend[...] = cinc[...]
        entry.start()
        inc[...] = mm(cinc[...], zh[...], zl[...]) + po_r[0:cols]
        exit_own[...] = local_e[...] + mm(inc[...], gh[...], gl[...])

        @pl.when(chip > 0)
        def _():
            ysend[...] = (
                pg_r[modes:] + mm(cinc[...], kh[...], kl[...]) + mm(exit_own[...], zh[...], zl[...], True)
            )
            for j in range(chips):
                @pl.when(j < chip)
                def _():
                    exit_to(j).start()

    incb[...] = mm(inc[...], uh[0], ul[0]) + off_a

    def settle(i, moving):
        following = []
        for k in range(2):
            s = k * half + i
            h, l = split(moving[k] + (srh[s].astype(F32) + srl[s].astype(F32)))
            adj[s] = rest[s] + mm_split(h, l, vh[s], vl[s])
            following.append(mm_split(h, l, fh[s], fl[s]))
            xh[s] = uh[s].T
            xl[s] = ul[s].T
        return tuple(following)

    lax.fori_loop(0, half, settle, (inc[...], incb[...]), unroll=4)

    def waves(b, carry):
        wg[b] = dot(wave[pl.ds(4 * b, 4)].reshape(4 * cols, modes), basis[...])
        return carry

    lax.fori_loop(0, slabs // 4, waves, 0)

    @pl.when(core == 1)
    def _():
        tiles = zsend[...]
        for k in range(1, groups):
            tile_to(k).wait_recv()
            tiles = tiles + zrecv[k]
        ssend[...] = tiles
        for d in range(n):
            @pl.when(me != d)
            def _():
                share_to(d).start()

        for j in range(chips - 2, 0, -1):
            @pl.when(chip < j)
            def _():
                wait_transfer(j)
                h, l = split(trecv[j].T)
                bh[j] = h
                bl[j] = l

        inc[...] = jnp.zeros_like(inc)
        for j in range(chips - 1, 0, -1):
            @pl.when(chip < j)
            def _():
                wait_exit(j)
                if j == chips - 1:
                    inc[...] = yrecv[j]
                else:
                    inc[...] = mm(inc[...], bh[j], bl[j]) + yrecv[j]

        jsend[...] = exit_own[...] + mm(inc[...], th[...], tl[...], True)
        joining.start()

    @pl.when(core == 0)
    def _():
        joining.wait_recv()
        inc[...] = jrecv[...]

    incb[...] = adj[half] + mm(inc[...], xh[half], xl[half])

    for b in range(slabs // 4):
        for i in range(4):
            s = 4 * b + i
            entering = incb if s < half else inc
            h, l = split(adj[s] + mm(entering[...], xh[s], xl[s]))
            ahl[b, cols * i : cols * (i + 1)] = h
            ahl[b, cols * (4 + i) : cols * (5 + i)] = l

    def products(slot, peer):
        columns = pl.ds(pl.multiple_of(peer * part, 128), part)
        points = basis[:, columns]
        for b in range(slabs // 4):
            ag = dot(ahl[b], points)
            both = wg[b, :, columns] * (ag[: 4 * cols] + ag[4 * cols :])
            for i in range(4):
                esend[slot, 4 * b + i : 4 * b + i + 1] = jnp.sum(
                    both[cols * i : cols * (i + 1)], axis=0, keepdims=True
                )

    copies = []
    low = 0
    high = groups - 1
    for slot in range(groups - 1):
        above = (high - mine >= mine - low).astype(jnp.int32)
        peer = above * high + (1 - above) * low
        low = low + 1 - above
        high = high - above
        products(slot, peer)
        at = lax.rem(peer + groups - mine, groups)
        copies.append(
            pltpu.make_async_remote_copy(
                src_ref=esend.at[slot], dst_ref=erecv.at[at],
                send_sem=es.at[slot], recv_sem=er.at[at],
                device_id=(peer, me), device_id_type=MESH,
            )
        )
        copies[-1].start()
    products(groups - 1, mine)

    @pl.when(core == 0)
    def _():
        cur[...] = jnp.zeros_like(cur)

    @pl.when(core == 1)
    def _():
        cur[...] = ssend[...]

    for j in range(chips):
        @pl.when(me != 2 * j + 1)
        def _():
            copy_to(ssend, srecv.at[j], ss.at[0], sr.at[j], other).wait_recv()
            cur[...] += srecv[j]

    current = jnp.sum(cur[...])
    factor = (all_slabs * grid * (2.0 / small)) / current
    for copy in copies:
        copy.wait_send()

    @pl.when(core == 0)
    def _():
        pair_off.wait_send()
        pair_u.wait_send()
        pair_g.wait_send()

    @pl.when(core == 1)
    def _():
        entry.wait_send()
        joining.wait_send()
        for k in range(1, groups):
            tile_to(k).wait_send()
        for d in range(n):
            @pl.when(me != d)
            def _():
                share_to(d).wait_send()

        @pl.when(onward)
        def _():
            offset_on.wait_send()

        @pl.when(jnp.logical_and(onward, chip > 0))
        def _():
            transfer_on.wait_send()

        @pl.when(jnp.logical_and(odd == 1, chip < chips - 1))
        def _():
            carried_to(0).wait_send()

            @pl.when(chip < chips - 2)
            def _():
                carried_to(1).wait_send()

        @pl.when(inner)
        def _():
            for j in range(chips):
                @pl.when(j < chip)
                def _():
                    transfer_to(j).wait_send()

        @pl.when(chip > 0)
        def _():
            for j in range(chips):
                @pl.when(j < chip)
                def _():
                    exit_to(j).wait_send()

    summed = esend[groups - 1]
    for k in range(1, groups):
        pltpu.make_async_remote_copy(
            src_ref=esend.at[0], dst_ref=erecv.at[k], send_sem=es.at[0], recv_sem=er.at[k],
            device_id=(mine, other), device_id_type=MESH,
        ).wait_recv()
        summed = summed + erecv[k]
    out[...] = summed * factor


def local(wavefunction, injected_modes, factor_blocks, pivot_inverse, mode_velocity, energy_weight, mode_basis):
    n = lax.axis_size("slab")
    groups = lax.axis_size("energy")
    _, slabs, cols, modes = wavefunction.shape
    grid = mode_basis.shape[1]
    part = grid // groups
    chips = n // 2
    vmem = pl.BlockSpec(memory_space=pltpu.VMEM)
    hbm = pl.BlockSpec(memory_space=pl.ANY)
    dma = pltpu.SemaphoreType.DMA

    def full(*shape):
        return pltpu.VMEM(shape, F32)

    def short(*shape):
        return pltpu.VMEM(shape, BF16)

    result = pl.pallas_call(
        functools.partial(kernel, n, groups),
        out_shape=jax.ShapeDtypeStruct((slabs, part), F32),
        in_specs=[vmem, vmem, hbm, hbm, vmem, vmem, vmem],
        out_specs=vmem,
        scratch_shapes=[
            full(2, slabs // 2, modes, modes),
            full(slabs, modes, modes),
            short(slabs // 4, 8 * cols, modes),
            dma((slabs,)),
            dma,
        ]
        + [short(slabs, modes, modes)] * 8
        + [short(modes, modes)] * 12
        + [short(chips, modes, modes)] * 2
        + [short(slabs, cols, modes)] * 2
        + [full(slabs, cols, modes)] * 2
        + [
            full(slabs // 4, 4 * cols, grid),
            full(2, cols, modes),
        ]
        + [full(cols, modes)] * 5
        + [full(cols, modes)] * 3
        + [full(8, 128)]
        + [full(cols + 8, modes)] * 2
        + [full(modes, modes)] * 2
        + [full(modes + cols, modes)] * 2
        + [full(cols, modes)] * 2
        + [
            full(modes, modes),
            full(chips, modes, modes),
            full(modes, modes),
        ]
        + [full(cols, modes)] * 2
        + [full(cols, modes)] * 2
        + [full(cols, modes), full(chips, cols, modes)]
        + [full(cols, modes)] * 2
        + [full(8, 128), full(groups, 8, 128)]
        + [full(8, 128), full(chips, 8, 128)]
        + [full(groups, slabs, part)] * 2
        + [dma] * 6
        + [dma] * 4
        + [dma((chips,))] * 2
        + [dma((2,)), dma]
        + [dma] * 2
        + [dma((chips,))] * 2
        + [dma] * 2
        + [dma((groups,))] * 2
        + [dma((n,)), dma((chips,))]
        + [dma((groups,))] * 2,
        compiler_params=pltpu.CompilerParams(
            collective_id=0, has_side_effects=True, vmem_limit_bytes=60 * 1024 * 1024
        ),
    )(
        wavefunction[0],
        injected_modes,
        factor_blocks.reshape(2, slabs // 2, modes, modes),
        pivot_inverse[0],
        mode_velocity,
        energy_weight.reshape(1, 1),
        mode_basis,
    )
    return result.T


def solution(mesh):
    return jax.shard_map(
        local,
        mesh=mesh,
        in_specs=(
            P("energy", "slab", None, None),
            P("energy", None),
            P("energy", "slab", None, None),
            P("energy", "slab", None, None),
            P("energy", None),
            P("energy"),
            P(),
        ),
        out_specs=P("energy", "slab"),
        check_vma=False,
    )
```
